32 devices in a mesh: grp: 2 (over x), row: 8 (over z, y), col: 2 (over core).
Axes of the slice: x: 2, y: 2, z: 4, core: 2. Of those that a mesh axis runs over, the one named last changes fastest.
Arguments:
- pair: bfloat16 [128, 64, 128], P(('grp', 'row'), 'col'), parts along dimension 0, may hold values from -6 to 6
- token_mask: int32 [128], P('grp'), parts along dimension 0, may hold values 0 or 1
- chain_ids: int32 [128], P('grp'), parts along dimension 0, may hold values from 0 to 5, as said below
- chain_bias: float32 [128], replicated, may hold values from -4 to 4
- in_gain: float32 [2, 128], replicated, may hold values from 0.5 to 2
- proj_weight: bfloat16 [2, 128, 640], replicated, may hold values from -0.5 to 0.5
- out_gain: float32 [2, 128], replicated, may hold values from 0.5 to 2
- out_weight: bfloat16 [2, 128, 128], replicated, may hold values from -0.5 to 0.5
Outputs:
- updated: bfloat16 [128, 64, 128], P(('grp', 'row'), 'col'), parts along dimension 0
The draws below stay inside these ranges and needn't reach their ends.
There are 2 independent parts, one for each index of `grp`. The reference program is written for one: setup_inputs(seed, part) draws one part's arguments, and reference() takes and returns one part's arrays. A program takes and returns all parts, laid end to end along the dimension named above; an argument that names none is the same for every part. Nothing has to cross between parts.
Inputs may be any that keep to these rules, and one draw needn't show every extreme that they name: `chain_ids`: chain ids never fall along the tokens; there are exactly six chains, each of at least one token.
All inputs are finite; a program needn't handle non-finite values.
Results may differ from the reference program's by a relative error of at most 0.012.
Values may be sent and summed in bfloat16 or wider, within the bound.
A program may use at most 64 MiB of HBM per device.

```python
import math
import jax
import jax.numpy as jnp
from jax import lax

WIDTH = 128
HIDDEN_SIZE = 128
TOKENS = 64


def draw_chain_ids(key, part):
    key = jax.random.fold_in(key, 7)
    order = jax.random.permutation(key, TOKENS - 1)
    cuts = order[:5].astype(jnp.int32) + 1
    positions = jnp.arange(TOKENS, dtype=jnp.int32)
    return jnp.sum((positions[:, None] >= cuts[None, :]).astype(jnp.int32), axis=1).astype(jnp.int32)


def touch_ends(values, key, least, largest):
    longest = values.shape.index(max(values.shape))
    spots = []
    for shift in (0, 1):
        where = [jax.random.randint(jax.random.fold_in(key, axis), (), 0, length) for axis, length in enumerate(values.shape)]
        where[longest] = (where[longest] + shift) % values.shape[longest]
        spots.append(tuple(where))
    return values.at[spots[0]].set(least).at[spots[1]].set(largest)


def levels(own_key, shape, split, least, largest):
    level = 1.0
    for position, shards_of in split:
        heights = jax.random.uniform(jax.random.fold_in(jax.random.fold_in(own_key, 6), position), (shards_of,), jnp.float32, least / len(split), largest / len(split))
        level = level * jnp.repeat(jnp.exp(heights), shape[position] // shards_of).reshape((-1,) + (1,) * (len(shape) - 1 - position))
    return level


def gaussian(key, extent, scale, bound, shards=(), kind=jnp.bfloat16):
    factor_of = levels(key, extent, shards, -0.22, 0.18) if shards else 1.0
    drawn = jax.random.normal(key, extent, jnp.float32) * scale * factor_of
    return jnp.minimum(jnp.maximum(drawn, -bound), bound).astype(kind)


def setup_inputs(seed: int = 0, part: int = 0) -> dict:
    arg_keys = jax.random.split(jax.random.key(seed), 9)
    part_splits = jax.random.split(jax.random.fold_in(arg_keys[8], part), 9)
    pair = gaussian(part_splits[0], (TOKENS, TOKENS, WIDTH), 1.0, 6.0, ((0, 8), (1, 2)))
    token_mask = touch_ends((jax.random.randint(part_splits[1], (TOKENS,), 0, 8) < 7).astype(jnp.int32), jax.random.fold_in(part_splits[1], 1), 0, 1)
    chain_ids = draw_chain_ids(jax.random.fold_in(jax.random.fold_in(arg_keys[8], part), 71), part)
    chain_bias = gaussian(arg_keys[3], (WIDTH,), 1.0, 4.0, (), jnp.float32)
    in_gain = jnp.clip(jnp.exp(jax.random.uniform(arg_keys[4], (2, WIDTH), jnp.float32, math.log(0.5), math.log(2.0))), 0.5, 2.0)
    proj_weight = gaussian(arg_keys[5], (2, WIDTH, 4 * HIDDEN_SIZE + WIDTH), WIDTH ** -0.5, 0.5)
    out_gain = jnp.clip(jnp.exp(jax.random.uniform(arg_keys[6], (2, HIDDEN_SIZE), jnp.float32, math.log(0.5), math.log(2.0))), 0.5, 2.0)
    out_weight = gaussian(arg_keys[7], (2, HIDDEN_SIZE, WIDTH), HIDDEN_SIZE ** -0.5, 0.5)
    return {"pair": pair, "token_mask": token_mask, "chain_ids": chain_ids, "chain_bias": chain_bias, "in_gain": in_gain, "proj_weight": proj_weight, "out_gain": out_gain, "out_weight": out_weight}


def layer_norm(values, gain):
    mean = lax.optimization_barrier(jnp.mean(values, axis=-1, keepdims=True))
    centred = values - mean
    variance = lax.optimization_barrier(jnp.mean(centred * centred, axis=-1, keepdims=True))
    return centred * lax.rsqrt(variance + 1e-05) * gain

def one_update(state, pmask, gain_in, weight_in, gain_out, weight_out, incoming):
    count, width = (state.shape[0], state.shape[2])
    hidden = weight_out.shape[0]
    normed = layer_norm(state, gain_in).astype(jnp.bfloat16)
    proj = jnp.dot(normed.reshape(-1, width), weight_in, preferred_element_type=jnp.float32)
    proj = proj.reshape(count, count, -1)
    a_side = (pmask[:, :, None] * jax.nn.sigmoid(proj[:, :, hidden:2 * hidden]) * proj[:, :, :hidden]).astype(jnp.bfloat16)
    b_side = (pmask[:, :, None] * jax.nn.sigmoid(proj[:, :, 3 * hidden:4 * hidden]) * proj[:, :, 2 * hidden:3 * hidden]).astype(jnp.bfloat16)
    gate = jax.nn.sigmoid(proj[:, :, 4 * hidden:])
    if incoming:
        mixed = jnp.einsum('kih,kjh->ijh', a_side.astype(jnp.float32), b_side.astype(jnp.float32))
    else:
        mixed = jnp.einsum('ikh,jkh->ijh', a_side.astype(jnp.float32), b_side.astype(jnp.float32))
    mnorm = layer_norm(mixed, gain_out).astype(jnp.bfloat16)
    change = jnp.dot(mnorm.reshape(-1, hidden), weight_out, preferred_element_type=jnp.float32).reshape(count, count, width)
    return (state + gate * change).astype(jnp.bfloat16)

def reference(pair, token_mask, chain_ids, chain_bias, in_gain, proj_weight, out_gain, out_weight):
    maskf = token_mask.astype(jnp.float32)
    pmask = maskf[:, None] * maskf[None, :]
    same = (chain_ids[:, None] == chain_ids[None, :]).astype(jnp.float32)
    start = pair.astype(jnp.float32) + same[:, :, None] * chain_bias
    first = one_update(start, pmask, in_gain[0], proj_weight[0], out_gain[0], out_weight[0], False)
    return one_update(first.astype(jnp.float32), pmask, in_gain[1], proj_weight[1], out_gain[1], out_weight[1], True)
```

```python
import functools
import jax
import jax.numpy as jnp
from jax import lax
from jax.experimental import pallas as pl
from jax.experimental.pallas import tpu as pltpu
from jax.sharding import PartitionSpec as P

F32 = jnp.float32
BF16 = jnp.bfloat16
MESH = pl.DeviceIdType.MESH


def sigmoid(x):
    return 0.5 * jnp.tanh(0.5 * x) + 0.5


def layer_norm(values, gain):
    mean = jnp.mean(values, axis=-1, keepdims=True)
    centred = values - mean
    variance = jnp.mean(centred * centred, axis=-1, keepdims=True)
    return centred * lax.rsqrt(variance + 1e-05) * gain


def kernel(
    nrow,
    pair_ref, mask_ref, chain_ref, bias_ref, gin_ref, wp_ref, gout_ref, wo_ref,
    out_ref,
    state, pm, gate, mixed, own_b, own_a, a1, a1f, b1, part, a2s, a2, b2,
    s_b1, s_f1, r_b1, s_a1, r_a1, s_a2, s_fa2, r_a2, s_b2, s_f2, r_b2,
):
    rows, cols, width = pair_ref.shape
    hidden = wo_ref.shape[1]
    nz = nrow // 2
    half = nrow // 2
    grp = lax.axis_index("grp")
    r = lax.axis_index("row")
    c = lax.axis_index("col")
    z, y = r // 2, r % 2
    rn = z * 2 + (1 - y)
    tokens = rows * cols
    d = r // half
    q_me = r % half

    def send(src, dst, ss, rs, row, col):
        return pltpu.make_async_remote_copy(
            src_ref=src, dst_ref=dst, send_sem=ss, recv_sem=rs,
            device_id=(grp, row, col), device_id_type=MESH,
        )

    barrier = pltpu.get_barrier_semaphore()
    for k in range(1, 2 * nrow):
        t = lax.rem(r * 2 + c + k, 2 * nrow)
        pl.semaphore_signal(barrier, inc=1, device_id=(grp, t // 2, t % 2), device_id_type=MESH)

    lane_rows = lax.broadcasted_iota(jnp.int32, (8, width), 0)
    for jb in range(cols // 8):
        mcol = jnp.zeros((8, width), jnp.int32)
        ccol = jnp.zeros((8, width), jnp.int32)
        for s in range(8):
            at = c * cols + jb * 8 + s
            mcol = jnp.where(lane_rows == s, mask_ref[at], mcol)
            ccol = jnp.where(lane_rows == s, chain_ref[at], ccol)
        mcol = mcol.astype(F32)
        js = slice(jb * 8, jb * 8 + 8)
        for i in range(rows):
            mi = mask_ref[r * rows + i].astype(F32)
            pm[i, js] = mcol * mi
            same = (ccol == chain_ref[r * rows + i]).astype(F32)
            state[i, js] = pair_ref[i, js].astype(F32) + same * bias_ref[...]

    def normed_of(l):
        zs = state[...].reshape(tokens, width)
        return layer_norm(zs, gin_ref[l : l + 1, :]).astype(BF16)

    def side(normed, l, at):
        pr = jnp.dot(normed, wp_ref[l, :, at : at + 2 * hidden], preferred_element_type=F32)
        return pm[...].reshape(tokens, width) * sigmoid(pr[:, hidden:]) * pr[:, :hidden]

    def gate_of(normed, l):
        pr = jnp.dot(normed, wp_ref[l, :, 4 * hidden :], preferred_element_type=F32)
        gate[...] = sigmoid(pr)

    def finish(l):
        mn = layer_norm(mixed[...].reshape(tokens, hidden), gout_ref[l : l + 1, :]).astype(BF16)
        change = jnp.dot(mn, wo_ref[l], preferred_element_type=F32)
        res = state[...].reshape(tokens, width) + gate[...] * change
        return res.astype(BF16)

    normed = normed_of(0)
    own_b[...] = side(normed, 0, 2 * hidden).astype(BF16).reshape(rows, cols, hidden)
    pl.semaphore_wait(barrier, 2 * nrow - 1)

    b_sends = []
    for dz in range(1, nz):
        tz = lax.rem(z + dz, nz)
        cp = send(own_b, b1.at[q_me, c], s_b1.at[dz], r_b1.at[q_me, c], tz * 2 + y, d)
        cp.start()
        b_sends.append(cp)
    sib_b = send(own_b, b1.at[q_me, c], s_b1.at[0], r_b1.at[q_me, c], r, 1 - c)

    @pl.when(d != c)
    def _():
        sib_b.start()

    @pl.when(d == c)
    def _():
        b1[q_me, c] = own_b[...]

    a1[c] = side(normed, 0, 0).astype(BF16).reshape(rows, cols, hidden)
    a_send = send(a1.at[c], a1.at[c], s_a1, r_a1, r, 1 - c)
    a_send.start()
    gate_of(normed, 0)

    f_sends = []
    for t in range(nz // 2):
        q = t * 2 + y
        mine = (c * (nz // 2) + t) == z
        for cc in range(2):
            @pl.when(jnp.logical_not(jnp.logical_and(mine, c == cc)))
            def _():
                send(b1.at[q, cc], b1.at[q, cc], s_b1.at[0], r_b1.at[q, cc], rn, c).wait_recv()
            cp = send(b1.at[q, cc], b1.at[q, cc], s_f1.at[t, cc], r_b1.at[q, cc], rn, c)
            cp.start()
            f_sends.append(cp)
        if t == 0:
            send(a1.at[1 - c], a1.at[1 - c], s_a1, r_a1, r, 1 - c).wait_recv()
            for cc in range(2):
                a1f[:, cc * cols : (cc + 1) * cols, :] = a1[cc].astype(F32)

    kb_n = 2 * cols // 8

    def outgoing(q):
        def body(j, carry):
            b0 = b1[q, 0, j].astype(F32)
            bb1 = b1[q, 1, j].astype(F32)
            bs = [b0[kb * 8 : kb * 8 + 8] for kb in range(kb_n // 2)]
            bs += [bb1[kb * 8 : kb * 8 + 8] for kb in range(kb_n // 2)]
            base = pl.multiple_of((q * rows + j) * (rows * 8), rows * 8)
            for i in range(rows):
                acc = a1f[i, 0:8] * bs[0]
                for kb in range(1, kb_n):
                    acc = acc + a1f[i, kb * 8 : kb * 8 + 8] * bs[kb]
                part[pl.ds(base + i * 8, 8), :] = acc
            return carry
        lax.fori_loop(0, rows, body, 0)

    for t in range(nz // 2):
        outgoing(t * 2 + y)
    for t in range(nz // 2):
        q = t * 2 + (1 - y)
        for cc in range(2):
            send(b1.at[q, cc], b1.at[q, cc], s_f1.at[t, cc], r_b1.at[q, cc], rn, c).wait_recv()
        outgoing(q)
    for i in range(rows):
        tot = part[pl.ds(i * 8, cols, stride=rows * 8), :]
        for s in range(1, 8):
            tot = tot + part[pl.ds(i * 8 + s, cols, stride=rows * 8), :]
        mixed[i] = tot
    state[...] = finish(0).astype(F32).reshape(rows, cols, width)

    normed = normed_of(1)
    a_side = side(normed, 1, 0).reshape(rows, cols, hidden)
    for q in range(half):
        a2s[q] = a_side[:, q * rows : (q + 1) * rows, :].reshape(rows * rows, hidden).astype(BF16)
    a_sends = []
    for k in range(half):
        q = lax.rem(q_me + k, half)
        tr = c * half + q
        cp = send(a2s.at[q], a2.at[r], s_a2.at[k], r_a2.at[r], tr, y)
        local = jnp.logical_and(tr == r, y == c)

        @pl.when(jnp.logical_not(local))
        def _():
            cp.start()

        @pl.when(local)
        def _():
            a2[r] = a2s[q]
        a_sends.append((cp, local))
    b2[r] = side(normed, 1, 2 * hidden).astype(BF16).reshape(rows, cols, hidden)
    b2_sends = []
    for dz in range(1, nz):
        tz = lax.rem(z + dz, nz)
        cp = send(b2.at[r], b2.at[r], s_b2.at[dz], r_b2.at[r], tz * 2 + y, c)
        cp.start()
        b2_sends.append(cp)
    cp = send(b2.at[r], b2.at[r], s_f2.at[0], r_b2.at[r], rn, c)
    cp.start()
    b2_sends.append(cp)
    gate_of(normed, 1)

    for t in range(nz):
        zz = lax.rem(z + t, nz)
        rr = zz * 2 + c
        @pl.when(jnp.logical_not(jnp.logical_and(rr == r, d == c)))
        def _():
            send(a2.at[rr], a2.at[rr], s_a2.at[0], r_a2.at[rr], r, 1 - c).wait_recv()
        cp = send(a2.at[rr], a2.at[rr], s_fa2.at[t], r_a2.at[rr], r, 1 - c)
        cp.start()
        b2_sends.append(cp)
    for t in range(nz):
        rr = lax.rem(z + t, nz) * 2 + (1 - c)
        send(a2.at[rr], a2.at[rr], s_fa2.at[t], r_a2.at[rr], r, 1 - c).wait_recv()

    jw = min(cols, 32)

    def incoming(rr, first):
        af = a2[rr].astype(F32)
        for jb in range(cols // jw):
            js = slice(jb * jw, (jb + 1) * jw)
            accs = [None if first else mixed[i, js] for i in range(rows)]
            for k in range(rows):
                bk = b2[rr, k, js].astype(F32)
                for i in range(rows):
                    term = af[k * rows + i : k * rows + i + 1, :] * bk
                    accs[i] = term if accs[i] is None else accs[i] + term
            for i in range(rows):
                mixed[i, js] = accs[i]

    incoming(r, True)
    for dz in range(1, nz):
        zz = lax.rem(z + nz - dz, nz)
        rr = zz * 2 + y
        send(b2.at[rr], b2.at[rr], s_b2.at[dz], r_b2.at[rr], rn, c).wait_recv()
        cp = send(b2.at[rr], b2.at[rr], s_f2.at[dz], r_b2.at[rr], rn, c)
        cp.start()
        b2_sends.append(cp)
        incoming(rr, False)
    for dz in range(nz):
        zz = lax.rem(z + nz - dz, nz)
        rr = zz * 2 + (1 - y)
        send(b2.at[rr], b2.at[rr], s_f2.at[dz], r_b2.at[rr], rn, c).wait_recv()
        incoming(rr, False)
    out_ref[...] = finish(1).reshape(rows, cols, width)

    for cp in b_sends + f_sends + b2_sends:
        cp.wait_send()
    a_send.wait_send()

    @pl.when(d != c)
    def _():
        sib_b.wait_send()

    for cp, local in a_sends:
        @pl.when(jnp.logical_not(local))
        def _():
            cp.wait_send()


def shards(nrow, pair, token_mask, chain_ids, chain_bias, in_gain, proj_weight, out_gain, out_weight):
    rows, cols, width = pair.shape
    hidden = out_weight.shape[1]
    half = nrow // 2
    nz = nrow // 2
    vm = pl.BlockSpec(memory_space=pltpu.VMEM)
    sm = pl.BlockSpec(memory_space=pltpu.SMEM)
    dma = pltpu.SemaphoreType.DMA
    block = (rows, cols, hidden)
    return pl.pallas_call(
        functools.partial(kernel, nrow),
        out_shape=jax.ShapeDtypeStruct(pair.shape, BF16),
        in_specs=[vm, sm, sm, vm, vm, vm, vm, vm],
        out_specs=vm,
        scratch_shapes=[
            pltpu.VMEM(pair.shape, F32),
            pltpu.VMEM((rows, cols, width), F32),
            pltpu.VMEM((rows * cols, width), F32),
            pltpu.VMEM(block, F32),
            pltpu.VMEM(block, BF16),
            pltpu.VMEM(block, BF16),
            pltpu.VMEM((2,) + block, BF16),
            pltpu.VMEM((rows, 2 * cols, hidden), F32),
            pltpu.VMEM((half, 2) + block, BF16),
            pltpu.VMEM((cols * rows * 8, hidden), F32),
            pltpu.VMEM((half, rows * rows, hidden), BF16),
            pltpu.VMEM((nrow, rows * rows, hidden), BF16),
            pltpu.VMEM((nrow,) + block, BF16),
            dma((nz,)), dma((nz // 2, 2)), dma((half, 2)), dma, dma,
            dma((half,)), dma((nz,)), dma((nrow,)),
            dma((nz,)), dma((nz,)), dma((nrow,)),
        ],
        compiler_params=pltpu.CompilerParams(
            collective_id=0, has_side_effects=True, vmem_limit_bytes=56 * 2**20
        ),
    )(pair, token_mask, chain_ids, chain_bias.reshape(1, width), in_gain, proj_weight, out_gain, out_weight)


def solution(mesh):
    in_specs = (P(("grp", "row"), "col", None), P("grp"), P("grp"), P(), P(), P(), P(), P())
    out_specs = P(("grp", "row"), "col", None)
    return jax.shard_map(
        functools.partial(shards, mesh.shape["row"]),
        mesh=mesh, in_specs=in_specs, out_specs=out_specs, check_vma=False,
    )
```

```python
import functools
import jax
import jax.numpy as jnp
from jax import lax
from jax.experimental import pallas as pl
from jax.experimental.pallas import tpu as pltpu
from jax.sharding import PartitionSpec as P

F32 = jnp.float32
BF16 = jnp.bfloat16
MESH = pl.DeviceIdType.MESH


def sigmoid(x):
    return 0.5 * jnp.tanh(0.5 * x) + 0.5


def layer_norm(values, gain):
    mean = jnp.mean(values, axis=-1, keepdims=True)
    centred = values - mean
    variance = jnp.mean(centred * centred, axis=-1, keepdims=True)
    return centred * lax.rsqrt(variance + 1e-05) * gain


def kernel(
    nrow,
    pair_ref, mask_ref, chain_ref, bias_ref, gin_ref, wp_ref, gout_ref, wo_ref,
    out_ref,
    state, pm, gate, mixed, own_b, a1, a1f, b1, part, ret, a2s, a2, b2, near, ret2,
    s_b1, r_b1, s_a1, r_a1, s_ret, r_ret, s_a2, s_fa2, r_a2, s_b2, r_b2,
):
    rows, cols, width = pair_ref.shape
    hidden = wo_ref.shape[1]
    nz = nrow // 2
    half = nrow // 2
    grp = lax.axis_index("grp")
    r = lax.axis_index("row")
    c = lax.axis_index("col")
    z, y = r // 2, r % 2
    rn = z * 2 + (1 - y)
    tokens = rows * cols
    d = r // half
    nt = nz // 2
    t_me = z % nt

    def send(src, dst, ss, rs, row, col):
        return pltpu.make_async_remote_copy(
            src_ref=src, dst_ref=dst, send_sem=ss, recv_sem=rs,
            device_id=(grp, row, col), device_id_type=MESH,
        )

    barrier = pltpu.get_barrier_semaphore()

    def greet(row, col):
        pl.semaphore_signal(barrier, inc=1, device_id=(grp, row, col), device_id_type=MESH)

    greet(r, 1 - c)
    greet(rn, c)
    for dz in range(1, nz):
        tz = lax.rem(z + dz, nz)
        greet(tz * 2 + y, c)

        @pl.when((tz * 2 + y) // half == c)
        def _():
            greet(tz * 2 + y, 1 - c)

    peers = 2 + (nz - 1) * jnp.where(d == c, 1, 2)

    lane_rows = lax.broadcasted_iota(jnp.int32, (8, width), 0)
    for jb in range(cols // 8):
        mcol = jnp.zeros((8, width), jnp.int32)
        ccol = jnp.zeros((8, width), jnp.int32)
        for s in range(8):
            at = c * cols + jb * 8 + s
            mcol = jnp.where(lane_rows == s, mask_ref[at], mcol)
            ccol = jnp.where(lane_rows == s, chain_ref[at], ccol)
        mcol = mcol.astype(F32)
        js = slice(jb * 8, jb * 8 + 8)
        for i in range(rows):
            mi = mask_ref[r * rows + i].astype(F32)
            pm[i, js] = mcol * mi
            same = (ccol == chain_ref[r * rows + i]).astype(F32)
            state[i, js] = pair_ref[i, js].astype(F32) + same * bias_ref[...]

    def normed_of(l):
        zs = state[...].reshape(tokens, width)
        return layer_norm(zs, gin_ref[l : l + 1, :]).astype(BF16)

    def side(normed, l, at):
        pr = jnp.dot(normed, wp_ref[l, :, at : at + 2 * hidden], preferred_element_type=F32)
        return pm[...].reshape(tokens, width) * sigmoid(pr[:, hidden:]) * pr[:, :hidden]

    def gate_of(normed, l):
        pr = jnp.dot(normed, wp_ref[l, :, 4 * hidden :], preferred_element_type=F32)
        gate[...] = sigmoid(pr)

    def finish(l):
        mn = layer_norm(mixed[...].reshape(tokens, hidden), gout_ref[l : l + 1, :]).astype(BF16)
        change = jnp.dot(mn, wo_ref[l], preferred_element_type=F32)
        res = state[...].reshape(tokens, width) + gate[...] * change
        return res.astype(BF16)

    normed = normed_of(0)
    own_b[...] = side(normed, 0, 2 * hidden).astype(BF16).reshape(rows, cols, hidden)
    pl.semaphore_wait(barrier, peers)

    sends = []
    for dz in range(1, nz):
        tz = lax.rem(z + dz, nz)
        cp = send(own_b, b1.at[t_me, c], s_b1.at[dz], r_b1.at[t_me, c], tz * 2 + y, d)
        cp.start()
        sends.append(cp)
    sib_b = send(own_b, b1.at[t_me, c], s_b1.at[0], r_b1.at[t_me, c], r, 1 - c)

    @pl.when(d != c)
    def _():
        sib_b.start()

    @pl.when(d == c)
    def _():
        b1[t_me, c] = own_b[...]

    a1[0, c] = side(normed, 0, 0).astype(BF16).reshape(rows, cols, hidden)
    near_a = send(a1.at[0, c], a1.at[1, c], s_a1.at[0], r_a1.at[0], rn, c)
    near_a.start()
    own_a = send(a1.at[0, c], a1.at[0, c], s_a1.at[1], r_a1.at[1], r, 1 - c)
    own_a.start()
    gate_of(normed, 0)
    near_a.wait_recv()
    far_a = send(a1.at[1, c], a1.at[1, c], s_a1.at[2], r_a1.at[2], r, 1 - c)
    far_a.start()
    sends += [near_a, own_a, far_a]
    own_a.wait_recv()
    far_a.wait_recv()
    for p in range(2):
        for cc in range(2):
            a1f[p, :, cc * cols : (cc + 1) * cols, :] = a1[p, cc].astype(F32)

    kb_n = 2 * cols // 8
    nj = nt * rows

    def outgoing(p, t):
        def body(j, carry):
            b0 = b1[t, 0, j].astype(F32)
            bb1 = b1[t, 1, j].astype(F32)
            bs = [b0[kb * 8 : kb * 8 + 8] for kb in range(kb_n // 2)]
            bs += [bb1[kb * 8 : kb * 8 + 8] for kb in range(kb_n // 2)]
            base = pl.multiple_of((t * rows + j) * (rows * 8), rows * 8)
            for i in range(rows):
                acc = a1f[p, i, 0:8] * bs[0]
                for kb in range(1, kb_n):
                    acc = acc + a1f[p, i, kb * 8 : kb * 8 + 8] * bs[kb]
                part[p, pl.ds(base + i * 8, 8), :] = acc
            return carry
        lax.fori_loop(0, rows, body, 0)

    def total(p, i):
        tot = part[p, pl.ds(i * 8, nj, stride=rows * 8), :]
        for k in range(1, 8):
            tot = tot + part[p, pl.ds(i * 8 + k, nj, stride=rows * 8), :]
        return tot

    for k in range(nt):
        t = lax.rem(t_me + k, nt)
        mine = (c * nt + t) == z
        for cc in range(2):
            @pl.when(jnp.logical_not(jnp.logical_and(mine, c == cc)))
            def _():
                send(b1.at[t, cc], b1.at[t, cc], s_b1.at[0], r_b1.at[t, cc], rn, c).wait_recv()
        outgoing(1, t)
    for i in range(rows):
        ret[0, i] = total(1, i).astype(BF16)
    back = send(ret.at[0], ret.at[1], s_ret.at[0], r_ret.at[0], rn, c)
    back.start()
    sends.append(back)
    for t in range(nt):
        outgoing(0, t)
    for i in range(rows):
        tot = total(0, i)
        for t in range(nt):
            at = pl.multiple_of((t * 2 + y) * rows, rows)
            mixed[i, pl.ds(at, rows)] = tot[t * rows : (t + 1) * rows]
    back.wait_recv()
    for i in range(rows):
        tot = ret[1, i].astype(F32)
        for t in range(nt):
            at = pl.multiple_of((t * 2 + 1 - y) * rows, rows)
            mixed[i, pl.ds(at, rows)] = tot[t * rows : (t + 1) * rows]
    state[...] = finish(0).astype(F32).reshape(rows, cols, width)

    normed = normed_of(1)
    a_side = side(normed, 1, 0).reshape(rows, cols, hidden)
    sq = rows * rows
    for t in range(nt):
        for p in range(2):
            q = t * 2 + p
            a2s[t, p * sq : (p + 1) * sq] = (
                a_side[:, q * rows : (q + 1) * rows, :].reshape(sq, hidden).astype(BF16)
            )
    a_sends = []
    for k in range(nt):
        t = lax.rem(t_me + k, nt)
        tz = c * nt + t
        cp = send(a2s.at[t], a2.at[z], s_a2.at[k], r_a2.at[z], tz * 2 + y, c)

        @pl.when(tz != z)
        def _():
            cp.start()

        @pl.when(tz == z)
        def _():
            a2[z] = a2s[t]
        a_sends.append((cp, tz != z))
    b2[z] = side(normed, 1, 2 * hidden).astype(BF16).reshape(rows, cols, hidden)
    for dz in range(1, nz):
        tz = lax.rem(z + dz, nz)
        cp = send(b2.at[z], b2.at[z], s_b2.at[dz], r_b2.at[z], tz * 2 + y, c)
        cp.start()
        sends.append(cp)
    gate_of(normed, 1)

    def hop(t):
        zz = lax.rem(z + t, nz)
        return send(a2.at[zz], a2.at[zz], s_fa2.at[t], r_a2.at[zz], r, 1 - c)

    @pl.when(d == c)
    def _():
        for t in range(nz):
            if t:
                hop(t).wait_recv()
            hop(t).start()

    @pl.when(d != c)
    def _():
        for t in range(nz):
            hop(t).wait_recv()

    jw = min(cols, 32)

    def incoming(dst, p, zz, first):
        af = a2[zz, pl.ds(pl.multiple_of(p * sq, sq), sq)].astype(F32)
        for jb in range(cols // jw):
            js = slice(jb * jw, (jb + 1) * jw)
            accs = [None if first else dst[i, js] for i in range(rows)]
            for k in range(rows):
                bk = b2[zz, k, js].astype(F32)
                for i in range(rows):
                    term = af[k * rows + i : k * rows + i + 1, :] * bk
                    accs[i] = term if accs[i] is None else accs[i] + term
            for i in range(rows):
                dst[i, js] = accs[i]

    for dz in range(nz):
        zz = lax.rem(z + nz - dz, nz)
        if dz:
            send(b2.at[zz], b2.at[zz], s_b2.at[dz], r_b2.at[zz], rn, c).wait_recv()
        incoming(near, 1 - y, zz, dz == 0)
        if dz < nz - 1:
            incoming(mixed, y, zz, dz == 0)
    ret2[0] = near[...].astype(BF16)
    back2 = send(ret2.at[0], ret2.at[1], s_ret.at[1], r_ret.at[1], rn, c)
    back2.start()
    sends.append(back2)
    incoming(mixed, y, lax.rem(z + 1, nz), False)
    back2.wait_recv()
    mixed[...] = mixed[...] + ret2[1].astype(F32)
    out_ref[...] = finish(1).reshape(rows, cols, width)

    for cp in sends:
        cp.wait_send()

    @pl.when(d != c)
    def _():
        sib_b.wait_send()

    @pl.when(d == c)
    def _():
        for t in range(nz):
            hop(t).wait_send()

    for cp, remote in a_sends:
        @pl.when(remote)
        def _():
            cp.wait_send()


def shards(nrow, pair, token_mask, chain_ids, chain_bias, in_gain, proj_weight, out_gain, out_weight):
    rows, cols, width = pair.shape
    hidden = out_weight.shape[1]
    nz = nrow // 2
    nt = nz // 2
    vm = pl.BlockSpec(memory_space=pltpu.VMEM)
    sm = pl.BlockSpec(memory_space=pltpu.SMEM)
    dma = pltpu.SemaphoreType.DMA
    block = (rows, cols, hidden)
    return pl.pallas_call(
        functools.partial(kernel, nrow),
        out_shape=jax.ShapeDtypeStruct(pair.shape, BF16),
        in_specs=[vm, sm, sm, vm, vm, vm, vm, vm],
        out_specs=vm,
        scratch_shapes=[
            pltpu.VMEM(pair.shape, F32),
            pltpu.VMEM((rows, cols, width), F32),
            pltpu.VMEM((rows * cols, width), F32),
            pltpu.VMEM(block, F32),
            pltpu.VMEM(block, BF16),
            pltpu.VMEM((2, 2) + block, BF16),
            pltpu.VMEM((2, rows, 2 * cols, hidden), F32),
            pltpu.VMEM((nt, 2) + block, BF16),
            pltpu.VMEM((2, nt * rows * rows * 8, hidden), F32),
            pltpu.VMEM((2, rows, nt * rows, hidden), BF16),
            pltpu.VMEM((nt, 2 * rows * rows, hidden), BF16),
            pltpu.VMEM((nz, 2 * rows * rows, hidden), BF16),
            pltpu.VMEM((nz,) + block, BF16),
            pltpu.VMEM(block, F32),
            pltpu.VMEM((2,) + block, BF16),
            dma((nz,)), dma((nt, 2)), dma((3,)), dma((3,)), dma((2,)), dma((2,)),
            dma((nt,)), dma((nz,)), dma((nz,)),
            dma((nz,)), dma((nz,)),
        ],
        compiler_params=pltpu.CompilerParams(
            collective_id=0, has_side_effects=True, vmem_limit_bytes=56 * 2**20
        ),
    )(pair, token_mask, chain_ids, chain_bias.reshape(1, width), in_gain, proj_weight, out_gain, out_weight)


def solution(mesh):
    in_specs = (P(("grp", "row"), "col", None), P("grp"), P("grp"), P(), P(), P(), P(), P())
    out_specs = P(("grp", "row"), "col", None)
    return jax.shard_map(
        functools.partial(shards, mesh.shape["row"]),
        mesh=mesh, in_specs=in_specs, out_specs=out_specs, check_vma=False,
    )
```

```python
import functools
import jax
import jax.numpy as jnp
from jax import lax
from jax.experimental import pallas as pl
from jax.experimental.pallas import tpu as pltpu
from jax.sharding import PartitionSpec as P

F32 = jnp.float32
BF16 = jnp.bfloat16
MESH = pl.DeviceIdType.MESH


def sigmoid(x):
    return 0.5 * jnp.tanh(0.5 * x) + 0.5


def layer_norm(values, gain):
    mean = jnp.mean(values, axis=-1, keepdims=True)
    centred = values - mean
    variance = jnp.mean(centred * centred, axis=-1, keepdims=True)
    return centred * lax.rsqrt(variance + 1e-05) * gain


def kernel(
    nrow,
    pair_ref, mask_ref, chain_ref, bias_ref, gin_ref, wp_ref, gout_ref, wo_ref,
    out_ref,
    state, pm, gate, mixed, own_b, a1, a1f, b1, part, ret, a2s, a2, b2, near, ret2,
    s_b1, r_b1, s_a1, r_a1, s_ret, r_ret, s_a2, s_fa2, r_a2, s_b2, r_b2,
):
    rows, cols, width = pair_ref.shape
    hidden = wo_ref.shape[1]
    nz = nrow // 2
    half = nrow // 2
    grp = lax.axis_index("grp")
    r = lax.axis_index("row")
    c = lax.axis_index("col")
    z, y = r // 2, r % 2
    rn = z * 2 + (1 - y)
    tokens = rows * cols
    d = r // half
    nt = nz // 2
    t_me = z % nt

    def send(src, dst, ss, rs, row, col):
        return pltpu.make_async_remote_copy(
            src_ref=src, dst_ref=dst, send_sem=ss, recv_sem=rs,
            device_id=(grp, row, col), device_id_type=MESH,
        )

    barrier = pltpu.get_barrier_semaphore()

    def greet(row, col):
        pl.semaphore_signal(barrier, inc=1, device_id=(grp, row, col), device_id_type=MESH)

    greet(r, 1 - c)
    greet(rn, c)
    for dz in range(1, nz):
        tz = lax.rem(z + dz, nz)
        greet(tz * 2 + y, c)

        @pl.when((tz * 2 + y) // half == c)
        def _():
            greet(tz * 2 + y, 1 - c)

    peers = 2 + (nz - 1) * jnp.where(d == c, 1, 2)

    lane_rows = lax.broadcasted_iota(jnp.int32, (8, width), 0)
    for jb in range(cols // 8):
        mcol = jnp.zeros((8, width), jnp.int32)
        ccol = jnp.zeros((8, width), jnp.int32)
        for s in range(8):
            at = c * cols + jb * 8 + s
            mcol = jnp.where(lane_rows == s, mask_ref[at], mcol)
            ccol = jnp.where(lane_rows == s, chain_ref[at], ccol)
        mcol = mcol.astype(F32)
        js = slice(jb * 8, jb * 8 + 8)
        for i in range(rows):
            mi = mask_ref[r * rows + i].astype(F32)
            pm[i, js] = mcol * mi
            same = (ccol == chain_ref[r * rows + i]).astype(F32)
            state[i, js] = pair_ref[i, js].astype(F32) + same * bias_ref[...]

    def normed_of(l):
        zs = state[...].reshape(tokens, width)
        return layer_norm(zs, gin_ref[l : l + 1, :]).astype(BF16)

    def side(normed, l, at):
        pr = jnp.dot(normed, wp_ref[l, :, at : at + 2 * hidden], preferred_element_type=F32)
        return pm[...].reshape(tokens, width) * sigmoid(pr[:, hidden:]) * pr[:, :hidden]

    def gate_of(normed, l):
        pr = jnp.dot(normed, wp_ref[l, :, 4 * hidden :], preferred_element_type=F32)
        gate[...] = sigmoid(pr)

    def finish(l):
        mn = layer_norm(mixed[...].reshape(tokens, hidden), gout_ref[l : l + 1, :]).astype(BF16)
        change = jnp.dot(mn, wo_ref[l], preferred_element_type=F32)
        res = state[...].reshape(tokens, width) + gate[...] * change
        return res.astype(BF16)

    normed = normed_of(0)
    own_b[...] = side(normed, 0, 2 * hidden).astype(BF16).reshape(rows, cols, hidden)
    pl.semaphore_wait(barrier, peers)

    sends = []
    for dz in range(1, nz):
        tz = lax.rem(z + dz, nz)
        cp = send(own_b, b1.at[t_me, c], s_b1.at[dz], r_b1.at[t_me, c], tz * 2 + y, d)
        cp.start()
        sends.append(cp)
    sib_b = send(own_b, b1.at[t_me, c], s_b1.at[0], r_b1.at[t_me, c], r, 1 - c)

    @pl.when(d != c)
    def _():
        sib_b.start()

    @pl.when(d == c)
    def _():
        b1[t_me, c] = own_b[...]

    a1[0, c] = side(normed, 0, 0).astype(BF16).reshape(rows, cols, hidden)
    near_a = send(a1.at[0, c], a1.at[1, c], s_a1.at[0], r_a1.at[0], rn, c)
    near_a.start()
    own_a = send(a1.at[0, c], a1.at[0, c], s_a1.at[1], r_a1.at[1], r, 1 - c)
    own_a.start()
    gate_of(normed, 0)
    near_a.wait_recv()
    far_a = send(a1.at[1, c], a1.at[1, c], s_a1.at[2], r_a1.at[2], r, 1 - c)
    far_a.start()
    sends += [near_a, own_a, far_a]
    own_a.wait_recv()
    far_a.wait_recv()
    for p in range(2):
        for cc in range(2):
            a1f[p, :, cc * cols : (cc + 1) * cols, :] = a1[p, cc].astype(F32)

    kb_n = 2 * cols // 8
    nj = nt * rows

    def outgoing(p, t):
        def body(j, carry):
            b0 = b1[t, 0, j].astype(F32)
            bb1 = b1[t, 1, j].astype(F32)
            bs = [b0[kb * 8 : kb * 8 + 8] for kb in range(kb_n // 2)]
            bs += [bb1[kb * 8 : kb * 8 + 8] for kb in range(kb_n // 2)]
            base = pl.multiple_of((t * rows + j) * (rows * 8), rows * 8)
            for i in range(rows):
                acc = a1f[p, i, 0:8] * bs[0]
                for kb in range(1, kb_n):
                    acc = acc + a1f[p, i, kb * 8 : kb * 8 + 8] * bs[kb]
                part[p, pl.ds(base + i * 8, 8), :] = acc
            return carry
        lax.fori_loop(0, rows, body, 0)

    def total(p, i):
        tot = part[p, pl.ds(i * 8, nj, stride=rows * 8), :]
        for k in range(1, 8):
            tot = tot + part[p, pl.ds(i * 8 + k, nj, stride=rows * 8), :]
        return tot

    for k in range(nt):
        t = lax.rem(t_me + k, nt)
        mine = (c * nt + t) == z
        for cc in range(2):
            @pl.when(jnp.logical_not(jnp.logical_and(mine, c == cc)))
            def _():
                send(b1.at[t, cc], b1.at[t, cc], s_b1.at[0], r_b1.at[t, cc], rn, c).wait_recv()
        outgoing(1, t)
    for i in range(rows):
        ret[0, i] = total(1, i).astype(BF16)
    back = send(ret.at[0], ret.at[1], s_ret.at[0], r_ret.at[0], rn, c)
    back.start()
    sends.append(back)
    for t in range(nt):
        outgoing(0, t)
    for i in range(rows):
        tot = total(0, i)
        for t in range(nt):
            at = pl.multiple_of((t * 2 + y) * rows, rows)
            mixed[i, pl.ds(at, rows)] = tot[t * rows : (t + 1) * rows]
    back.wait_recv()
    for i in range(rows):
        tot = ret[1, i].astype(F32)
        for t in range(nt):
            at = pl.multiple_of((t * 2 + 1 - y) * rows, rows)
            mixed[i, pl.ds(at, rows)] = tot[t * rows : (t + 1) * rows]
    state[...] = finish(0).astype(F32).reshape(rows, cols, width)

    normed = normed_of(1)
    a_side = side(normed, 1, 0).reshape(rows, cols, hidden)
    sq = rows * rows
    for t in range(nt):
        for p in range(2):
            q = t * 2 + p
            a2s[t, p * sq : (p + 1) * sq] = (
                a_side[:, q * rows : (q + 1) * rows, :].reshape(sq, hidden).astype(BF16)
            )
    a_sends = []
    for k in range(nt):
        t = lax.rem(t_me + k, nt)
        tz = c * nt + t
        cp = send(a2s.at[t], a2.at[z], s_a2.at[k], r_a2.at[z], tz * 2 + y, c)

        @pl.when(tz != z)
        def _():
            cp.start()

        @pl.when(tz == z)
        def _():
            a2[z] = a2s[t]
        a_sends.append((cp, tz != z))
    hc = cols // 2
    b_side = side(normed, 1, 2 * hidden).reshape(rows, cols, hidden)
    for h in range(2):
        b2[z, h] = b_side[:, h * hc : (h + 1) * hc, :].astype(BF16)
    for h in range(2):
        for dz in range(1, nz):
            tz = lax.rem(z + dz, nz)
            cp = send(b2.at[z, h], b2.at[z, h], s_b2.at[dz, h], r_b2.at[z, h], tz * 2 + y, c)
            cp.start()
            sends.append(cp)
    gate_of(normed, 1)

    def hop(t):
        zz = lax.rem(z + t, nz)
        return send(a2.at[zz], a2.at[zz], s_fa2.at[t], r_a2.at[zz], r, 1 - c)

    @pl.when(d == c)
    def _():
        for t in range(nz):
            if t:
                hop(t).wait_recv()
            hop(t).start()

    @pl.when(d != c)
    def _():
        for t in range(nz):
            hop(t).wait_recv()

    jw = min(hc, 32)

    def incoming(dst, p, zz, h, first):
        af = a2[zz, pl.ds(pl.multiple_of(p * sq, sq), sq)].astype(F32)
        for jb in range(hc // jw):
            js = slice(jb * jw, (jb + 1) * jw)
            to = slice(h * hc + jb * jw, h * hc + (jb + 1) * jw)
            accs = [None if first else dst[i, to] for i in range(rows)]
            for k in range(rows):
                bk = b2[zz, h, k, js].astype(F32)
                for i in range(rows):
                    term = af[k * rows + i : k * rows + i + 1, :] * bk
                    accs[i] = term if accs[i] is None else accs[i] + term
            for i in range(rows):
                dst[i, to] = accs[i]

    backs = []
    for h in range(2):
        for dz in range(nz):
            zz = lax.rem(z + nz - dz, nz)
            if dz:
                send(b2.at[zz, h], b2.at[zz, h], s_b2.at[dz, h], r_b2.at[zz, h], rn, c).wait_recv()
            incoming(near, 1 - y, zz, h, dz == 0)
        ret2[0, h] = near[:, h * hc : (h + 1) * hc, :].astype(BF16)
        back2 = send(ret2.at[0, h], ret2.at[1, h], s_ret.at[1 + h], r_ret.at[1 + h], rn, c)
        back2.start()
        sends.append(back2)
        backs.append(back2)
        for dz in range(nz):
            incoming(mixed, y, lax.rem(z + nz - dz, nz), h, dz == 0)
    for h in range(2):
        to = slice(h * hc, (h + 1) * hc)
        backs[h].wait_recv()
        mixed[:, to, :] = mixed[:, to, :] + ret2[1, h].astype(F32)
    out_ref[...] = finish(1).reshape(rows, cols, width)

    for cp in sends:
        cp.wait_send()

    @pl.when(d != c)
    def _():
        sib_b.wait_send()

    @pl.when(d == c)
    def _():
        for t in range(nz):
            hop(t).wait_send()

    for cp, remote in a_sends:
        @pl.when(remote)
        def _():
            cp.wait_send()


def shards(nrow, pair, token_mask, chain_ids, chain_bias, in_gain, proj_weight, out_gain, out_weight):
    rows, cols, width = pair.shape
    hidden = out_weight.shape[1]
    nz = nrow // 2
    nt = nz // 2
    vm = pl.BlockSpec(memory_space=pltpu.VMEM)
    sm = pl.BlockSpec(memory_space=pltpu.SMEM)
    dma = pltpu.SemaphoreType.DMA
    block = (rows, cols, hidden)
    return pl.pallas_call(
        functools.partial(kernel, nrow),
        out_shape=jax.ShapeDtypeStruct(pair.shape, BF16),
        in_specs=[vm, sm, sm, vm, vm, vm, vm, vm],
        out_specs=vm,
        scratch_shapes=[
            pltpu.VMEM(pair.shape, F32),
            pltpu.VMEM((rows, cols, width), F32),
            pltpu.VMEM((rows * cols, width), F32),
            pltpu.VMEM(block, F32),
            pltpu.VMEM(block, BF16),
            pltpu.VMEM((2, 2) + block, BF16),
            pltpu.VMEM((2, rows, 2 * cols, hidden), F32),
            pltpu.VMEM((nt, 2) + block, BF16),
            pltpu.VMEM((2, nt * rows * rows * 8, hidden), F32),
            pltpu.VMEM((2, rows, nt * rows, hidden), BF16),
            pltpu.VMEM((nt, 2 * rows * rows, hidden), BF16),
            pltpu.VMEM((nz, 2 * rows * rows, hidden), BF16),
            pltpu.VMEM((nz, 2, rows, cols // 2, hidden), BF16),
            pltpu.VMEM(block, F32),
            pltpu.VMEM((2, 2, rows, cols // 2, hidden), BF16),
            dma((nz,)), dma((nt, 2)), dma((3,)), dma((3,)), dma((3,)), dma((3,)),
            dma((nt,)), dma((nz,)), dma((nz,)),
            dma((nz, 2)), dma((nz, 2)),
        ],
        compiler_params=pltpu.CompilerParams(
            collective_id=0, has_side_effects=True, vmem_limit_bytes=56 * 2**20
        ),
    )(pair, token_mask, chain_ids, chain_bias.reshape(1, width), in_gain, proj_weight, out_gain, out_weight)


def solution(mesh):
    in_specs = (P(("grp", "row"), "col", None), P("grp"), P("grp"), P(), P(), P(), P(), P())
    out_specs = P(("grp", "row"), "col", None)
    return jax.shard_map(
        functools.partial(shards, mesh.shape["row"]),
        mesh=mesh, in_specs=in_specs, out_specs=out_specs, check_vma=False,
    )
```

```python
import functools
import jax
import jax.numpy as jnp
from jax import lax
from jax.experimental import pallas as pl
from jax.experimental.pallas import tpu as pltpu
from jax.sharding import PartitionSpec as P

F32 = jnp.float32
BF16 = jnp.bfloat16
MESH = pl.DeviceIdType.MESH


def sigmoid(x):
    return 0.5 * jnp.tanh(0.5 * x) + 0.5


def layer_norm(values, gain):
    mean = jnp.mean(values, axis=-1, keepdims=True)
    centred = values - mean
    variance = jnp.mean(centred * centred, axis=-1, keepdims=True)
    return centred * lax.rsqrt(variance + 1e-05) * gain


def kernel(
    nrow,
    pair_ref, mask_ref, chain_ref, bias_ref, gin_ref, wp_ref, gout_ref, wo_ref,
    out_ref,
    state, pm, gate, mixed, own_b, a1, a1f, b1, part, ret, a2s, a2, b2, near, ret2,
    s_b1, r_b1, s_a1, r_a1, s_ret, r_ret, s_a2, s_fa2, r_a2, s_b2, r_b2,
):
    rows, cols, width = pair_ref.shape
    hidden = wo_ref.shape[1]
    nz = nrow // 2
    half = nrow // 2
    grp = lax.axis_index("grp")
    r = lax.axis_index("row")
    c = lax.axis_index("col")
    z, y = r // 2, r % 2
    rn = z * 2 + (1 - y)
    tokens = rows * cols
    d = r // half
    nt = nz // 2
    t_me = z % nt

    def send(src, dst, ss, rs, row, col):
        return pltpu.make_async_remote_copy(
            src_ref=src, dst_ref=dst, send_sem=ss, recv_sem=rs,
            device_id=(grp, row, col), device_id_type=MESH,
        )

    barrier = pltpu.get_barrier_semaphore()

    def greet(row, col):
        pl.semaphore_signal(barrier, inc=1, device_id=(grp, row, col), device_id_type=MESH)

    greet(r, 1 - c)
    greet(rn, c)
    for dz in range(1, nz):
        tz = lax.rem(z + dz, nz)
        greet(tz * 2 + y, c)

        @pl.when((tz * 2 + y) // half == c)
        def _():
            greet(tz * 2 + y, 1 - c)

    peers = 2 + (nz - 1) * jnp.where(d == c, 1, 2)

    lane_rows = lax.broadcasted_iota(jnp.int32, (8, width), 0)
    for jb in range(cols // 8):
        mcol = jnp.zeros((8, width), jnp.int32)
        ccol = jnp.zeros((8, width), jnp.int32)
        for s in range(8):
            at = c * cols + jb * 8 + s
            mcol = jnp.where(lane_rows == s, mask_ref[at], mcol)
            ccol = jnp.where(lane_rows == s, chain_ref[at], ccol)
        mcol = mcol.astype(F32)
        js = slice(jb * 8, jb * 8 + 8)
        for i in range(rows):
            mi = mask_ref[r * rows + i].astype(F32)
            pm[i, js] = mcol * mi
            same = (ccol == chain_ref[r * rows + i]).astype(F32)
            state[i, js] = pair_ref[i, js].astype(F32) + same * bias_ref[...]

    def normed_of(l):
        zs = state[...].reshape(tokens, width)
        return layer_norm(zs, gin_ref[l : l + 1, :]).astype(BF16)

    def side(normed, l, at):
        pr = jnp.dot(normed, wp_ref[l, :, at : at + 2 * hidden], preferred_element_type=F32)
        return pm[...].reshape(tokens, width) * sigmoid(pr[:, hidden:]) * pr[:, :hidden]

    def gate_of(normed, l):
        pr = jnp.dot(normed, wp_ref[l, :, 4 * hidden :], preferred_element_type=F32)
        gate[...] = sigmoid(pr)

    def finish(l):
        mn = layer_norm(mixed[...].reshape(tokens, hidden), gout_ref[l : l + 1, :]).astype(BF16)
        change = jnp.dot(mn, wo_ref[l], preferred_element_type=F32)
        res = state[...].reshape(tokens, width) + gate[...] * change
        return res.astype(BF16)

    normed = normed_of(0)
    own_b[...] = side(normed, 0, 2 * hidden).astype(BF16).reshape(rows, cols, hidden)
    a1[0, c] = side(normed, 0, 0).astype(BF16).reshape(rows, cols, hidden)
    gate_of(normed, 0)
    pl.semaphore_wait(barrier, peers)

    sends = []
    for dz in range(1, nz):
        tz = lax.rem(z + dz, nz)
        cp = send(own_b, b1.at[t_me, c], s_b1.at[dz], r_b1.at[t_me, c], tz * 2 + y, d)
        cp.start()
        sends.append(cp)
    sib_b = send(own_b, b1.at[t_me, c], s_b1.at[0], r_b1.at[t_me, c], r, 1 - c)

    @pl.when(d != c)
    def _():
        sib_b.start()

    @pl.when(d == c)
    def _():
        b1[t_me, c] = own_b[...]

    near_a = send(a1.at[0, c], a1.at[1, c], s_a1.at[0], r_a1.at[0], rn, c)
    near_a.start()
    own_a = send(a1.at[0, c], a1.at[0, c], s_a1.at[1], r_a1.at[1], r, 1 - c)
    own_a.start()
    near_a.wait_recv()
    far_a = send(a1.at[1, c], a1.at[1, c], s_a1.at[2], r_a1.at[2], r, 1 - c)
    far_a.start()
    sends += [near_a, own_a, far_a]
    own_a.wait_recv()
    far_a.wait_recv()
    for p in range(2):
        for cc in range(2):
            a1f[p, :, cc * cols : (cc + 1) * cols, :] = a1[p, cc].astype(F32)

    kb_n = 2 * cols // 8
    nj = nt * rows

    def outgoing(p, t):
        def body(j, carry):
            b0 = b1[t, 0, j].astype(F32)
            bb1 = b1[t, 1, j].astype(F32)
            bs = [b0[kb * 8 : kb * 8 + 8] for kb in range(kb_n // 2)]
            bs += [bb1[kb * 8 : kb * 8 + 8] for kb in range(kb_n // 2)]
            base = pl.multiple_of((t * rows + j) * (rows * 8), rows * 8)
            for i in range(rows):
                acc = a1f[p, i, 0:8] * bs[0]
                for kb in range(1, kb_n):
                    acc = acc + a1f[p, i, kb * 8 : kb * 8 + 8] * bs[kb]
                part[p, pl.ds(base + i * 8, 8), :] = acc
            return carry
        lax.fori_loop(0, rows, body, 0)

    def total(p, i):
        tot = part[p, pl.ds(i * 8, nj, stride=rows * 8), :]
        for k in range(1, 8):
            tot = tot + part[p, pl.ds(i * 8 + k, nj, stride=rows * 8), :]
        return tot

    for k in range(nt):
        t = lax.rem(t_me + k, nt)
        mine = (c * nt + t) == z
        for cc in range(2):
            @pl.when(jnp.logical_not(jnp.logical_and(mine, c == cc)))
            def _():
                send(b1.at[t, cc], b1.at[t, cc], s_b1.at[0], r_b1.at[t, cc], rn, c).wait_recv()
        outgoing(1, t)
    for i in range(rows):
        ret[0, i] = total(1, i).astype(BF16)
    back = send(ret.at[0], ret.at[1], s_ret.at[0], r_ret.at[0], rn, c)
    back.start()
    sends.append(back)
    for t in range(nt):
        outgoing(0, t)
    for i in range(rows):
        tot = total(0, i)
        for t in range(nt):
            at = pl.multiple_of((t * 2 + y) * rows, rows)
            mixed[i, pl.ds(at, rows)] = tot[t * rows : (t + 1) * rows]
    back.wait_recv()
    for i in range(rows):
        tot = ret[1, i].astype(F32)
        for t in range(nt):
            at = pl.multiple_of((t * 2 + 1 - y) * rows, rows)
            mixed[i, pl.ds(at, rows)] = tot[t * rows : (t + 1) * rows]
    state[...] = finish(0).astype(F32).reshape(rows, cols, width)

    normed = normed_of(1)
    a_side = side(normed, 1, 0).reshape(rows, cols, hidden)
    sq = rows * rows
    for t in range(nt):
        for p in range(2):
            q = t * 2 + p
            a2s[t, p * sq : (p + 1) * sq] = (
                a_side[:, q * rows : (q + 1) * rows, :].reshape(sq, hidden).astype(BF16)
            )
    a_sends = []
    for k in range(nt):
        t = lax.rem(t_me + k, nt)
        tz = c * nt + t
        cp = send(a2s.at[t], a2.at[z], s_a2.at[k], r_a2.at[z], tz * 2 + y, c)

        @pl.when(tz != z)
        def _():
            cp.start()

        @pl.when(tz == z)
        def _():
            a2[z] = a2s[t]
        a_sends.append((cp, tz != z))
    hc = cols // 2
    b_side = side(normed, 1, 2 * hidden).reshape(rows, cols, hidden)
    for h in range(2):
        b2[z, h] = b_side[:, h * hc : (h + 1) * hc, :].astype(BF16)
    for h in range(2):
        for dz in range(1, nz):
            tz = lax.rem(z + dz, nz)
            cp = send(b2.at[z, h], b2.at[z, h], s_b2.at[dz, h], r_b2.at[z, h], tz * 2 + y, c)
            cp.start()
            sends.append(cp)
    gate_of(normed, 1)

    def hop(t):
        zz = lax.rem(z + t, nz)
        return send(a2.at[zz], a2.at[zz], s_fa2.at[t], r_a2.at[zz], r, 1 - c)

    @pl.when(d == c)
    def _():
        for t in range(nz):
            if t:
                hop(t).wait_recv()
            hop(t).start()

    @pl.when(d != c)
    def _():
        for t in range(nz):
            hop(t).wait_recv()

    jw = min(hc, 32)

    def incoming(dst, p, zz, h, first):
        af = a2[zz, pl.ds(pl.multiple_of(p * sq, sq), sq)].astype(F32)
        for jb in range(hc // jw):
            js = slice(jb * jw, (jb + 1) * jw)
            to = slice(h * hc + jb * jw, h * hc + (jb + 1) * jw)
            accs = [None if first else dst[i, to] for i in range(rows)]
            for k in range(rows):
                bk = b2[zz, h, k, js].astype(F32)
                for i in range(rows):
                    term = af[k * rows + i : k * rows + i + 1, :] * bk
                    accs[i] = term if accs[i] is None else accs[i] + term
            for i in range(rows):
                dst[i, to] = accs[i]

    backs = []
    for h in range(2):
        for dz in range(nz):
            zz = lax.rem(z + nz - dz, nz)
            if dz:
                send(b2.at[zz, h], b2.at[zz, h], s_b2.at[dz, h], r_b2.at[zz, h], rn, c).wait_recv()
            incoming(near, 1 - y, zz, h, dz == 0)
        ret2[0, h] = near[:, h * hc : (h + 1) * hc, :].astype(BF16)
        back2 = send(ret2.at[0, h], ret2.at[1, h], s_ret.at[1 + h], r_ret.at[1 + h], rn, c)
        back2.start()
        sends.append(back2)
        backs.append(back2)
        for dz in range(nz):
            incoming(mixed, y, lax.rem(z + nz - dz, nz), h, dz == 0)
    for h in range(2):
        to = slice(h * hc, (h + 1) * hc)
        backs[h].wait_recv()
        mixed[:, to, :] = mixed[:, to, :] + ret2[1, h].astype(F32)
    out_ref[...] = finish(1).reshape(rows, cols, width)

    for cp in sends:
        cp.wait_send()

    @pl.when(d != c)
    def _():
        sib_b.wait_send()

    @pl.when(d == c)
    def _():
        for t in range(nz):
            hop(t).wait_send()

    for cp, remote in a_sends:
        @pl.when(remote)
        def _():
            cp.wait_send()


def shards(nrow, pair, token_mask, chain_ids, chain_bias, in_gain, proj_weight, out_gain, out_weight):
    rows, cols, width = pair.shape
    hidden = out_weight.shape[1]
    nz = nrow // 2
    nt = nz // 2
    vm = pl.BlockSpec(memory_space=pltpu.VMEM)
    sm = pl.BlockSpec(memory_space=pltpu.SMEM)
    dma = pltpu.SemaphoreType.DMA
    block = (rows, cols, hidden)
    return pl.pallas_call(
        functools.partial(kernel, nrow),
        out_shape=jax.ShapeDtypeStruct(pair.shape, BF16),
        in_specs=[vm, sm, sm, vm, vm, vm, vm, vm],
        out_specs=vm,
        scratch_shapes=[
            pltpu.VMEM(pair.shape, F32),
            pltpu.VMEM((rows, cols, width), F32),
            pltpu.VMEM((rows * cols, width), F32),
            pltpu.VMEM(block, F32),
            pltpu.VMEM(block, BF16),
            pltpu.VMEM((2, 2) + block, BF16),
            pltpu.VMEM((2, rows, 2 * cols, hidden), F32),
            pltpu.VMEM((nt, 2) + block, BF16),
            pltpu.VMEM((2, nt * rows * rows * 8, hidden), F32),
            pltpu.VMEM((2, rows, nt * rows, hidden), BF16),
            pltpu.VMEM((nt, 2 * rows * rows, hidden), BF16),
            pltpu.VMEM((nz, 2 * rows * rows, hidden), BF16),
            pltpu.VMEM((nz, 2, rows, cols // 2, hidden), BF16),
            pltpu.VMEM(block, F32),
            pltpu.VMEM((2, 2, rows, cols // 2, hidden), BF16),
            dma((nz,)), dma((nt, 2)), dma((3,)), dma((3,)), dma((3,)), dma((3,)),
            dma((nt,)), dma((nz,)), dma((nz,)),
            dma((nz, 2)), dma((nz, 2)),
        ],
        compiler_params=pltpu.CompilerParams(
            collective_id=0, has_side_effects=True, vmem_limit_bytes=56 * 2**20
        ),
    )(pair, token_mask, chain_ids, chain_bias.reshape(1, width), in_gain, proj_weight, out_gain, out_weight)


def solution(mesh):
    in_specs = (P(("grp", "row"), "col", None), P("grp"), P("grp"), P(), P(), P(), P(), P())
    out_specs = P(("grp", "row"), "col", None)
    return jax.shard_map(
        functools.partial(shards, mesh.shape["row"]),
        mesh=mesh, in_specs=in_specs, out_specs=out_specs, check_vma=False,
    )
```
